256 devices in a mesh: member: 16 (over y_lo, x, core), fsdp: 16 (over y_hi, z).
Axes of the slice: x: 4, y: 4 (y_hi: 2, y_lo: 2; y = y_hi * 2 + y_lo), z: 8, core: 2. Of those that a mesh axis runs over, the one named last changes fastest.
Arguments:
- analysis: float32 [16, 12, 16, 16, 1024], P('member', None, 'fsdp'), may hold values from -6 to 6
- owner: int32 [1], replicated, may hold values from 0 to 15
- noise: bfloat16 [128, 12, 16, 16, 1024], P('member', None, 'fsdp'), may hold values from -4 to 4
- depth_weight: float32 [3, 3, 1024], replicated, may hold values from -2 to 2
- depth_bias: float32 [1024], replicated, may hold values from -3 to 3
- norm_gain: float32 [1024], replicated, may hold values from 0.1 to 1.9
- up_weight: bfloat16 [1024, 2048], P('fsdp'), may hold values from -0.1875 to 0.1875
- up_bias: float32 [2048], replicated, may hold values from -3 to 3
- down_weight: bfloat16 [2048, 1024], P('fsdp'), may hold values from -0.125 to 0.125
- down_bias: float32 [1024], replicated, may hold values from -3 to 3
Outputs:
- block_out: bfloat16 [128, 12, 16, 16, 1024], P('member', None, 'fsdp')
The draws below stay inside these ranges and needn't reach their ends.
All inputs are finite; a program needn't handle non-finite values.
Results may differ from the reference program's by a relative error of at most 0.0054.
Values may be sent and summed in bfloat16 or wider, within the bound.
A program may use at most 128 MiB of HBM per device.

```python
import jax
import jax.numpy as jnp
import numpy as np
from jax import lax

C = 1024
HID = 2048
FACES = 12
FSIDE = 16
MEMBERS = 128
N_MEMBER = 16


def block_levels(own_key, extent, shards, smallest, top_value):
    gain = 1.0
    for dim, blocks in shards:
        heights = jax.random.uniform(jax.random.fold_in(jax.random.fold_in(own_key, 6), dim), (blocks,), jnp.float32, smallest / len(shards), top_value / len(shards))
        gain = gain * jnp.repeat(jnp.exp(heights), extent[dim] // blocks).reshape((-1,) + (1,) * (len(extent) - 1 - dim))
    return gain


def bell_draw(own_key, shape, scale, bound, split=(), kind=jnp.bfloat16):
    values = scale * jax.random.normal(own_key, shape, jnp.float32)
    if split:
        values = values * block_levels(own_key, shape, split, -0.22, 0.18)
    return jnp.clip(values, -bound, bound).astype(kind)


def setup_inputs(seed: int = 0) -> dict:
    key_of = jax.random.split(jax.random.key(seed), 11)
    return {
        "analysis": bell_draw(key_of[0], (N_MEMBER, FACES, FSIDE, FSIDE, C), 1.0, 6.0, ((0, 16), (2, 16)), jnp.float32),
        "owner": jax.random.randint(key_of[1], (1,), 0, N_MEMBER).astype(jnp.int32),
        "noise": bell_draw(key_of[2], (MEMBERS, FACES, FSIDE, FSIDE, C), 0.5, 4.0, ((0, 16), (2, 16))),
        "depth_weight": bell_draw(key_of[3], (3, 3, C), 9 ** -0.5, 2.0, (), jnp.float32),
        "depth_bias": bell_draw(key_of[4], (C,), 0.5, 3.0, (), jnp.float32),
        "norm_gain": jnp.clip(1.0 + 0.18 * jax.random.normal(key_of[5], (C,), jnp.float32), 0.1, 1.9),
        "up_weight": bell_draw(key_of[6], (C, HID), C ** -0.5, 0.1875, ((0, 16),)),
        "up_bias": bell_draw(key_of[7], (HID,), 0.5, 3.0, (), jnp.float32),
        "down_weight": bell_draw(key_of[8], (HID, C), HID ** -0.5, 0.125, ((0, 16),)),
        "down_bias": bell_draw(key_of[9], (C,), 0.5, 3.0, (), jnp.float32),
    }


up_table = np.array([(f + 4) % 12 for f in range(12)], dtype=np.int32)
down_table = np.array([(f + 8) % 12 for f in range(12)], dtype=np.int32)
left_table = np.array([4 * (f // 4) + (f + 3) % 4 for f in range(12)], dtype=np.int32)
right_table = np.array([4 * (f // 4) + (f + 1) % 4 for f in range(12)], dtype=np.int32)

def face_pad(field):
    side = field.shape[1]
    rows = jnp.concatenate([field[up_table][:, side - 1:side], field, field[down_table][:, 0:1]], axis=1)
    return jnp.concatenate([rows[left_table][:, :, side - 1:side], rows, rows[right_table][:, :, 0:1]], axis=2)

def reference(analysis, owner, noise, depth_weight, depth_bias, norm_gain, up_weight, up_bias, down_weight, down_bias):
    state = lax.dynamic_index_in_dim(analysis, owner[0], 0, keepdims=False)

    def one_member(noise_member):
        start = (state + noise_member.astype(jnp.float32)).astype(jnp.bfloat16)
        padded = face_pad(start)
        conv = jnp.zeros(start.shape, jnp.float32) + depth_bias
        for i in range(3):
            for j in range(3):
                conv = conv + depth_weight[i, j] * padded[:, i:i + FSIDE, j:j + FSIDE].astype(jnp.float32)
        mean = lax.optimization_barrier(jnp.mean(conv, axis=-1, keepdims=True))
        var = lax.optimization_barrier(jnp.mean(jnp.square(conv - mean), axis=-1, keepdims=True))
        normed = ((conv - mean) * lax.rsqrt(var + 1e-06) * norm_gain).astype(jnp.bfloat16)
        flat = normed.reshape(-1, C)
        upper = jnp.dot(flat, up_weight, preferred_element_type=jnp.float32) + up_bias
        hidden = jax.nn.gelu(upper, approximate=True).astype(jnp.bfloat16)
        lower = jnp.dot(hidden, down_weight, preferred_element_type=jnp.float32) + down_bias
        return (start.reshape(-1, C).astype(jnp.float32) + lower).astype(jnp.bfloat16).reshape(start.shape)
    return lax.map(one_member, noise)
```

```python
import functools

import jax
import jax.numpy as jnp
from jax import lax
from jax.experimental import pallas as pl
from jax.experimental.pallas import tpu as pltpu
from jax.sharding import PartitionSpec as P

GROUPS = 3
MEM = 8
UNITS = GROUPS * MEM
RING = 64
C = 1024
HID = 2048
PER_BATCH = 4
BATCHES = UNITS // PER_BATCH
ROWS = PER_BATCH * RING
HALF = C // 2
SLICE = GROUPS * RING // 4
UP_W = HID // 8
DN_W = C // 8
MESH = pl.DeviceIdType.MESH


def gelu(v):
    return 0.5 * v * (1.0 + jnp.tanh(0.7978845608028654 * (v + 0.044715 * (v * v * v))))


def kernel(
    owner_ref, analysis, noise, dw, db, gain, wu, ub, wd, bd, out,
    own, halo_up, halo_dn, normed, wup, wdn, st, pair, pick, xs_buf, ys_buf, conv, hid,
    halo_s, halo_r, zs, zr, ys, yr, xs, xr, cs, cr, a_s, a_r, local,
):
    m = lax.axis_index("member")
    p = lax.axis_index("fsdp")
    core = lax.rem(m, 2)
    x = lax.rem(lax.div(m, 2), 4)
    yl = lax.div(m, 8)
    yh = lax.div(p, 8)
    z = lax.rem(p, 8)
    y = yh * 2 + yl
    sib_core = 1 - core

    def dev(mm, pp):
        return {"member": mm, "fsdp": pp}

    def zdev(k):
        return dev(m, yh * 8 + lax.rem(z + k, 8))

    def xdev(k):
        return dev(yl * 8 + lax.rem(x + k, 4) * 2 + core, p)

    def ypos(k):
        q = lax.rem(y + k, 4)
        return lax.div(q, 2), lax.rem(q, 2)

    def ydev(k):
        h, l = ypos(k)
        return dev(l * 8 + x * 2 + core, h * 8 + z)

    sib = dev(yl * 8 + x * 2 + sib_core, p)
    nxt = dev(m, lax.rem(p + 1, 16))
    prv = dev(m, lax.rem(p + 15, 16))

    def rc(src, dst, s, r, d):
        return pltpu.make_async_remote_copy(
            src_ref=src, dst_ref=dst, send_sem=s, recv_sem=r, device_id=d, device_id_type=MESH
        )

    barrier = pltpu.get_barrier_semaphore()
    partners = [zdev(k) for k in range(1, 8)] + [nxt, prv] + [xdev(k) for k in (1, 2, 3)]
    partners += [ydev(1), ydev(3), sib]
    for d in partners:
        pl.semaphore_signal(barrier, inc=1, device_id=d, device_id_type=MESH)
    pl.semaphore_wait(barrier, len(partners))

    waits = []

    def send(desc):
        desc.start()
        waits.append(desc)

    def ch(cc):
        return pl.ds(pl.multiple_of(cc * HALF, HALF), HALF)

    def up_cols(xx, cc):
        return pl.ds(pl.multiple_of((xx * 2 + cc) * UP_W, UP_W), UP_W)

    def dn_cols(xx, cc):
        return pl.ds(pl.multiple_of((xx * 2 + cc) * DN_W, DN_W), DN_W)

    def srows(xx):
        return pl.ds(pl.multiple_of(xx * SLICE, SLICE), SLICE)

    send(rc(analysis.at[:, ch(sib_core)], pair.at[core], a_s.at[0], a_r.at[0], sib))
    c_pair = pltpu.make_async_copy(analysis.at[:, ch(core)], pair.at[core], local.at[0])
    c_pair.start()

    up_own, dn_own = up_cols(x, core), dn_cols(x, core)
    for k in range(1, 8):
        send(rc(wu.at[yl, :, up_own], wup.at[yh, z, yl, :, up_own], zs.at[0, k - 1], zr.at[0, k - 1], zdev(k)))
    for k in range(1, 8):
        send(rc(wd.at[yl, :, dn_own], wdn.at[yh, z, yl, :, dn_own], zs.at[1, k - 1], zr.at[1, k - 1], zdev(k)))
    c_up = pltpu.make_async_copy(wu.at[yl, :, up_own], wup.at[yh, z, yl, :, up_own], local.at[1])
    c_dn = pltpu.make_async_copy(wd.at[yl, :, dn_own], wdn.at[yh, z, yl, :, dn_own], local.at[2])
    c_own = pltpu.make_async_copy(noise, own, local.at[3])
    c_up.start()
    c_dn.start()
    c_own.start()

    first = p == 0
    last = p == 15

    def halo(u):
        g, mm = lax.div(u, MEM), lax.rem(u, MEM)
        g_up = jnp.where(last, lax.rem(g + 1, 3), g)
        g_dn = jnp.where(first, lax.rem(g + 2, 3), g)
        return (
            rc(noise.at[mm, g_up], halo_up.at[u], halo_s.at[0, u], halo_r.at[0, u], nxt),
            rc(noise.at[mm, g_dn], halo_dn.at[u], halo_s.at[1, u], halo_r.at[1, u], prv),
        )

    def start_halo(u, carry):
        a, b = halo(u)
        a.start()
        b.start()
        return carry

    lax.fori_loop(0, UNITS, start_halo, 0)

    owner = owner_ref[0]
    c_pair.wait()
    rc(pair.at[core], pair.at[sib_core], a_s.at[0], a_r.at[0], sib).wait_recv()
    pick[...] = pair[lax.rem(owner, 2)]
    for k in (1, 2, 3):
        xx = lax.rem(x + k, 4)
        send(rc(pick.at[srows(xx)], xs_buf.at[x], a_s.at[k], a_r.at[k], xdev(k)))
    xs_buf[x] = pick[srows(x)]
    for k in (1, 2, 3):
        rc(xs_buf.at[x], xs_buf.at[lax.rem(x + 4 - k, 4)], a_s.at[k], a_r.at[k], xdev(k)).wait_recv()
    ys_buf[yl] = xs_buf[lax.rem(lax.div(owner, 2), 4)]
    partner = dev((1 - yl) * 8 + x * 2 + core, p)
    send(rc(ys_buf.at[yl], ys_buf.at[yl], a_s.at[4], a_r.at[4], partner))
    rc(ys_buf.at[yl], ys_buf.at[1 - yl], a_s.at[4], a_r.at[4], partner).wait_recv()
    st[1, srows(x), ch(core)] = ys_buf[lax.div(owner, 8)]
    mine = st.at[1, srows(x), ch(core)]
    send(rc(mine, st.at[0, srows(x), ch(core)], a_s.at[5], a_r.at[5], nxt))
    send(rc(mine, st.at[2, srows(x), ch(core)], a_s.at[6], a_r.at[6], prv))

    def spread(row):
        here = st.at[row, srows(x), ch(core)]
        for k in (1, 2, 3):
            i = 7 + row * 3 + k - 1
            send(rc(here, here, a_s.at[i], a_r.at[i], xdev(k)))

    spread(1)

    c_up.wait()
    c_dn.wait()
    for k in range(1, 8):
        zz = lax.rem(z + 8 - k, 8)
        rc(wu.at[yl, :, up_own], wup.at[yh, zz, yl, :, up_own], zs.at[0, k - 1], zr.at[0, k - 1], zdev(k)).wait_recv()
        rc(wd.at[yl, :, dn_own], wdn.at[yh, zz, yl, :, dn_own], zs.at[1, k - 1], zr.at[1, k - 1], zdev(k)).wait_recv()

    def up_y(k):
        h, l = ypos(k)
        return wup.at[h, :, l, :, up_own]

    def dn_y(k):
        h, l = ypos(k)
        return wdn.at[h, :, l, :, dn_own]

    send(rc(up_y(0), up_y(0), ys.at[0], yr.at[0], ydev(1)))
    send(rc(up_y(0), up_y(0), ys.at[1], yr.at[1], ydev(3)))
    send(rc(dn_y(0), dn_y(0), ys.at[2], yr.at[2], ydev(1)))
    send(rc(dn_y(0), dn_y(0), ys.at[3], yr.at[3], ydev(3)))

    rc(mine, st.at[0, srows(x), ch(core)], a_s.at[5], a_r.at[5], nxt).wait_recv()
    spread(0)
    rc(mine, st.at[2, srows(x), ch(core)], a_s.at[6], a_r.at[6], prv).wait_recv()
    spread(2)

    rc(up_y(0), up_y(3), ys.at[0], yr.at[0], ydev(1)).wait_recv()
    send(rc(up_y(3), up_y(3), ys.at[4], yr.at[4], ydev(1)))
    rc(dn_y(0), dn_y(1), ys.at[3], yr.at[3], ydev(3)).wait_recv()
    send(rc(dn_y(1), dn_y(1), ys.at[5], yr.at[5], ydev(3)))

    def state_half(row, cc):
        return st.at[row, :, ch(cc)]

    for row in range(3):
        for k in (1, 2, 3):
            i = 7 + row * 3 + k - 1
            there = st.at[row, srows(lax.rem(x + 4 - k, 4)), ch(core)]
            rc(there, there, a_s.at[i], a_r.at[i], xdev(k)).wait_recv()
        send(rc(state_half(row, core), state_half(row, core), a_s.at[16 + row], a_r.at[16 + row], sib))

    def up_x(k, cc=core):
        return wup.at[:, :, :, :, up_cols(lax.rem(x + k, 4), cc)]

    def dn_x(k, cc=core):
        return wdn.at[:, :, :, :, dn_cols(lax.rem(x + k, 4), cc)]

    rc(up_y(0), up_y(1), ys.at[1], yr.at[1], ydev(3)).wait_recv()
    rc(up_y(0), up_y(2), ys.at[4], yr.at[4], ydev(1)).wait_recv()
    send(rc(up_x(0), up_x(0), xs.at[0], xr.at[0], xdev(1)))
    send(rc(up_x(0), up_x(0), xs.at[1], xr.at[1], xdev(3)))
    rc(dn_y(0), dn_y(3), ys.at[2], yr.at[2], ydev(1)).wait_recv()
    rc(dn_y(0), dn_y(2), ys.at[5], yr.at[5], ydev(3)).wait_recv()
    send(rc(dn_x(0), dn_x(0), xs.at[2], xr.at[2], xdev(1)))
    send(rc(dn_x(0), dn_x(0), xs.at[3], xr.at[3], xdev(3)))
    send(rc(up_x(0), up_x(0), cs.at[0, 0], cr.at[0, 0], sib))
    send(rc(dn_x(0), dn_x(0), cs.at[1, 0], cr.at[1, 0], sib))

    for row in range(3):
        rc(state_half(row, core), state_half(row, sib_core), a_s.at[16 + row], a_r.at[16 + row], sib).wait_recv()
    c_own.wait()

    def cells(u, carry):
        g, mm = lax.div(u, MEM), lax.rem(u, MEM)
        a, b = halo(u)
        a.wait_recv()
        b.wait_recv()
        g0 = pl.multiple_of(jnp.where(first, lax.rem(g + 1, 3), g) * RING, RING)
        g1 = pl.multiple_of(g * RING, RING)
        g2 = pl.multiple_of(jnp.where(last, lax.rem(g + 2, 3), g) * RING, RING)
        total = jnp.zeros((RING, 128), jnp.float32)
        for lane in range(C // 128):
            cols = pl.ds(lane * 128, 128)
            r0 = (st[0, pl.ds(g0, RING), cols] + halo_up[u, :, cols].astype(jnp.float32)).astype(jnp.bfloat16)
            r1 = (st[1, pl.ds(g1, RING), cols] + own[mm, g, :, cols].astype(jnp.float32)).astype(jnp.bfloat16)
            r2 = (st[2, pl.ds(g2, RING), cols] + halo_dn[u, :, cols].astype(jnp.float32)).astype(jnp.bfloat16)
            out[mm, g, :, cols] = r1
            rows = [r.astype(jnp.float32) for r in (r0, r1, r2)]
            parts = []
            for j in range(3):
                acc = rows[0] * dw[pl.ds(j, 1), cols]
                acc = acc + rows[1] * dw[pl.ds(3 + j, 1), cols]
                acc = acc + rows[2] * dw[pl.ds(6 + j, 1), cols]
                parts.append(acc)
            v = parts[1] + db[:, cols] + pltpu.roll(parts[0], 1, 0) + pltpu.roll(parts[2], RING - 1, 0)
            conv[:, cols] = v
            total = total + v
        mean = jnp.sum(total, axis=1, keepdims=True) * (1.0 / C)
        square = jnp.zeros((RING, 128), jnp.float32)
        for lane in range(C // 128):
            cols = pl.ds(lane * 128, 128)
            v = conv[:, cols] - mean
            square = square + v * v
        var = jnp.sum(square, axis=1, keepdims=True) * (1.0 / C)
        inv = lax.rsqrt(var + 1e-06)
        for lane in range(C // 128):
            cols = pl.ds(lane * 128, 128)
            v = (conv[:, cols] - mean) * inv * gain[:, cols]
            normed[pl.ds(pl.multiple_of(u * RING, RING), RING), cols] = v.astype(jnp.bfloat16)
        return carry

    def mlp(b, carry):
        rows = pl.ds(pl.multiple_of(b * ROWS, ROWS), ROWS)
        left = normed[rows, :]
        for n in range(4):
            cols = pl.ds(n * 512, 512)
            w = wup[:, :, :, :, cols].reshape(C, 512)
            t = jnp.dot(left, w, preferred_element_type=jnp.float32) + ub[:, cols]
            hid[:, cols] = gelu(t).astype(jnp.bfloat16)
        g = lax.div(b, 2)
        m0 = lax.rem(b, 2) * PER_BATCH
        h = hid[...]
        for n in range(2):
            cols = pl.ds(n * 512, 512)
            w = wdn[:, :, :, :, cols].reshape(HID, 512)
            t = jnp.dot(h, w, preferred_element_type=jnp.float32) + bd[:, cols]
            t = t.reshape(PER_BATCH, RING, 512)
            s = out[pl.ds(m0, PER_BATCH), g, :, cols].astype(jnp.float32)
            out[pl.ds(m0, PER_BATCH), g, :, cols] = (s + t).astype(jnp.bfloat16)
        return carry

    lax.fori_loop(0, 2 * PER_BATCH, cells, 0)

    rc(up_x(0), up_x(3), xs.at[0], xr.at[0], xdev(1)).wait_recv()
    send(rc(up_x(3), up_x(3), xs.at[4], xr.at[4], xdev(1)))
    send(rc(up_x(3), up_x(3), cs.at[0, 3], cr.at[0, 3], sib))
    rc(up_x(0), up_x(1), xs.at[1], xr.at[1], xdev(3)).wait_recv()
    send(rc(up_x(1), up_x(1), cs.at[0, 1], cr.at[0, 1], sib))
    rc(dn_x(0), dn_x(1), xs.at[3], xr.at[3], xdev(3)).wait_recv()
    send(rc(dn_x(1), dn_x(1), xs.at[5], xr.at[5], xdev(3)))
    send(rc(dn_x(1), dn_x(1), cs.at[1, 1], cr.at[1, 1], sib))
    rc(dn_x(0), dn_x(3), xs.at[2], xr.at[2], xdev(1)).wait_recv()
    send(rc(dn_x(3), dn_x(3), cs.at[1, 3], cr.at[1, 3], sib))

    lax.fori_loop(2 * PER_BATCH, 3 * PER_BATCH, cells, 0)

    rc(up_x(0), up_x(2), xs.at[4], xr.at[4], xdev(1)).wait_recv()
    send(rc(up_x(2), up_x(2), cs.at[0, 2], cr.at[0, 2], sib))
    rc(dn_x(0), dn_x(2), xs.at[5], xr.at[5], xdev(3)).wait_recv()
    send(rc(dn_x(2), dn_x(2), cs.at[1, 2], cr.at[1, 2], sib))
    for k in range(4):
        rc(up_x(k), up_x(k, sib_core), cs.at[0, k], cr.at[0, k], sib).wait_recv()
        rc(dn_x(k), dn_x(k, sib_core), cs.at[1, k], cr.at[1, k], sib).wait_recv()

    def step(b, carry):
        @pl.when(b >= 3)
        def _():
            lax.fori_loop(b * PER_BATCH, (b + 1) * PER_BATCH, cells, 0)

        return mlp(b, carry)

    lax.fori_loop(0, BATCHES, step, 0)

    for desc in waits:
        desc.wait_send()

    def end_halo(u, carry):
        a, b = halo(u)
        a.wait_send()
        b.wait_send()
        return carry

    lax.fori_loop(0, UNITS, end_halo, 0)


def shards(analysis, owner, noise, depth_weight, depth_bias, norm_gain, up_weight, up_bias, down_weight, down_bias):
    shape = noise.shape
    any_space = pl.BlockSpec(memory_space=pl.ANY)
    vmem = pl.BlockSpec(memory_space=pltpu.VMEM)
    dma = pltpu.SemaphoreType.DMA
    bf, f32 = jnp.bfloat16, jnp.float32
    result = pl.pallas_call(
        kernel,
        out_shape=jax.ShapeDtypeStruct((MEM, GROUPS, RING, C), bf),
        in_specs=[
            pl.BlockSpec(memory_space=pltpu.SMEM), any_space, any_space, vmem, vmem, vmem,
            any_space, vmem, any_space, vmem,
        ],
        out_specs=vmem,
        scratch_shapes=[
            pltpu.VMEM((MEM, GROUPS, RING, C), bf),
            pltpu.VMEM((UNITS, RING, C), bf),
            pltpu.VMEM((UNITS, RING, C), bf),
            pltpu.VMEM((UNITS * RING, C), bf),
            pltpu.VMEM((2, 8, 2, 32, HID), bf),
            pltpu.VMEM((2, 8, 2, 64, C), bf),
            pltpu.VMEM((3, GROUPS * RING, C), f32),
            pltpu.VMEM((2, GROUPS * RING, HALF), f32),
            pltpu.VMEM((GROUPS * RING, HALF), f32),
            pltpu.VMEM((4, SLICE, HALF), f32),
            pltpu.VMEM((2, SLICE, HALF), f32),
            pltpu.VMEM((RING, C), f32),
            pltpu.VMEM((ROWS, HID), bf),
            dma((2, UNITS)), dma((2, UNITS)),
            dma((2, 7)), dma((2, 7)),
            dma((6,)), dma((6,)),
            dma((6,)), dma((6,)),
            dma((2, 4)), dma((2, 4)),
            dma((19,)), dma((19,)),
            dma((4,)),
        ],
        compiler_params=pltpu.CompilerParams(
            collective_id=0, has_side_effects=True, vmem_limit_bytes=50 * 1024 * 1024
        ),
        name="block",
    )(
        owner,
        analysis.reshape(GROUPS * RING, C),
        noise.reshape(MEM, GROUPS, RING, C),
        depth_weight.reshape(9, C),
        depth_bias.reshape(1, C),
        norm_gain.reshape(1, C),
        up_weight.reshape(2, 32, HID),
        up_bias.reshape(1, HID),
        down_weight.reshape(2, 64, C),
        down_bias.reshape(1, C),
    )
    return result.reshape(shape)


def solution(mesh):
    placed = (
        P("member", None, "fsdp", None, None),
        P(),
        P("member", None, "fsdp", None, None),
        P(),
        P(),
        P(),
        P("fsdp", None),
        P(),
        P("fsdp", None),
        P(),
    )
    return jax.shard_map(
        shards,
        mesh=mesh,
        in_specs=placed,
        out_specs=P("member", None, "fsdp", None, None),
        check_vma=False,
    )
```
